256 devices in a mesh: replica: 16 (over x_lo, z), outer: 16 (over x_hi, y, core).
Axes of the slice: x: 4 (x_hi: 2, x_lo: 2; x = x_hi * 2 + x_lo), y: 4, z: 8, core: 2. Of those that a mesh axis runs over, the one named last changes fastest.
Arguments:
- tokens: bfloat16 [32768, 14848], P(('replica', 'outer')), may hold values from -24 to 24
- cotangent: bfloat16 [32768, 1024], P(('replica', 'outer')), may hold values from -3 to 3
- kv_weight: bfloat16 [14848, 1024], P('outer'), may hold values from -0.046875 to 0.046875
- gain: float32 [14848], replicated, may hold values from 0.25 to 2
- bias: float32 [14848], replicated, may hold values from -4 to 4
Outputs:
- grad_tokens: bfloat16 [32768, 14848], P(('replica', 'outer'))
- grad_weight: bfloat16 [14848, 1024], P('outer')
- grad_gain: float32 [14848], replicated
- grad_bias: float32 [14848], replicated
The draws below stay inside these ranges and needn't reach their ends.
All inputs are finite; a program needn't handle non-finite values.
Results may differ from the reference program's by a relative error of at most 0.0049.
Values may be sent and summed in bfloat16 or wider, within the bound.
A program may use at most 256 MiB of HBM per device.

```python
import jax
import jax.numpy as jnp
from jax import lax

D = 14848
TOK_DEV = 128
KVW = 1024
TOKENS = 32768
N_REPLICA = 16


def with_spikes(drawn, rng, source, target, parts, factor):
    owner, partner = [(jnp.arange(drawn.shape[axis_at]) // (drawn.shape[axis_at] // parts)).reshape([-1 if axis == axis_at else 1 for axis in range(drawn.ndim)]) for axis_at in (source, target)]
    chosen = jax.random.permutation(rng, parts)[partner]
    strong = (owner == chosen) | (owner == (partner + parts // 2) % parts)
    return jnp.where(strong, factor * drawn, drawn)


def shard_levels(own_key, extent, cuts, smallest, largest):
    def one(dim, blocks):
        steps = jax.random.uniform(jax.random.fold_in(jax.random.fold_in(own_key, 6), dim), (blocks,), jnp.float32, smallest / len(cuts), largest / len(cuts))
        return jnp.repeat(jnp.exp(steps), extent[dim] // blocks).reshape((-1,) + (1,) * (len(extent) - dim - 1))

    factor_of = one(*cuts[0])
    for cut in cuts[1:]:
        factor_of = factor_of * one(*cut)
    return factor_of


def gaussian(key, dims, deviation, most, cuts=(), kind=jnp.bfloat16):
    values = deviation * jax.random.normal(key, dims, jnp.float32)
    if cuts:
        values = values * shard_levels(key, dims, cuts, -0.22, 0.18)
    return jnp.clip(values, -most, most).astype(kind)


def noise_with(own_key, shape, scale, most, pieces, heavy, held_as=jnp.bfloat16):
    array = scale * jax.random.normal(own_key, shape, jnp.float32)
    if pieces:
        array = array * shard_levels(own_key, shape, pieces, -0.22, 0.18)
    return jnp.clip(with_spikes(array, jax.random.fold_in(own_key, 3), *heavy), -most, most).astype(held_as)


def setup_inputs(seed: int = 0) -> dict:
    key_of = jax.random.split(jax.random.key(seed), 6)
    tokens = noise_with(key_of[0], (TOKENS, D), 1.0, 24.0, ((0, 256),), (0, 1, 256, 6.0))
    cotangent = gaussian(key_of[1], (TOKENS, KVW), 0.5, 3.0, ((0, 256),))
    kv_weight = gaussian(key_of[2], (D, KVW), D ** -0.5, 0.046875, ((0, 16),))
    gain = jnp.clip(jax.random.uniform(key_of[3], (D,), jnp.float32, 0.25, 2.0), 0.25, 2.0)
    bias = gaussian(key_of[4], (D,), 1.0, 4.0, (), jnp.float32)
    return dict(tokens=tokens, cotangent=cotangent, kv_weight=kv_weight, gain=gain, bias=bias)


epsilon = 1e-05

def layer_stats(rows):
    values = rows.astype(jnp.float32)
    centre_mean = lax.optimization_barrier(jnp.mean(values, axis=1, keepdims=True))
    centre = values - centre_mean
    inv_std = lax.rsqrt(lax.optimization_barrier(jnp.mean(centre * centre, axis=1, keepdims=True)) + epsilon)
    return (centre * inv_std, inv_std)

def norm_backward(grad_hidden, normed, inv_std, gain):
    scaled = gain[None, :] * lax.optimization_barrier(grad_hidden).astype(jnp.float32)
    first = lax.optimization_barrier(jnp.mean(scaled, axis=1, keepdims=True))
    second = lax.optimization_barrier(jnp.mean(scaled * normed, axis=1, keepdims=True))
    return (inv_std * (scaled - first - normed * second)).astype(jnp.bfloat16)

def reference(tokens, cotangent, kv_weight, gain, bias):
    blocks = TOKENS // TOK_DEV

    def step(carry, index):
        acc_weight, acc_gain, acc_bias = carry
        start = (index * TOK_DEV).astype(jnp.int32)
        rows = lax.dynamic_slice_in_dim(tokens, start, TOK_DEV, 0)
        cot_rows = lax.dynamic_slice_in_dim(cotangent, start, TOK_DEV, 0)
        normed, inv_std = layer_stats(rows)
        hidden = (gain[None, :] * normed + bias[None, :]).astype(jnp.bfloat16)
        grad_hidden = lax.dot_general(cot_rows, kv_weight, (((1,), (1,)), ((), ())), preferred_element_type=jnp.float32).astype(jnp.bfloat16)
        grad_float = lax.optimization_barrier(grad_hidden).astype(jnp.float32)
        acc_weight = acc_weight + lax.dot_general(hidden, cot_rows, (((0,), (0,)), ((), ())), preferred_element_type=jnp.float32)
        acc_gain = acc_gain + lax.optimization_barrier(jnp.sum(grad_float * normed, axis=0))
        acc_bias = acc_bias + lax.optimization_barrier(jnp.sum(grad_float, axis=0))
        return ((acc_weight, acc_gain, acc_bias), norm_backward(grad_hidden, normed, inv_std, gain))
    start_carry = (jnp.zeros((D, KVW), jnp.float32), jnp.zeros((D,), jnp.float32), jnp.zeros((D,), jnp.float32))
    carry, grad_blocks = lax.scan(step, start_carry, jnp.arange(blocks, dtype=jnp.int32))
    grad_tokens = grad_blocks.reshape(TOKENS, D)
    return (grad_tokens, (carry[0] / N_REPLICA).astype(jnp.bfloat16), carry[1] / N_REPLICA, carry[2] / N_REPLICA)
```

```python
import jax
import jax.numpy as jnp
from jax import lax
from jax.experimental import pallas as pl
from jax.experimental.pallas import tpu as pltpu
from jax.sharding import PartitionSpec as P

BF = jnp.bfloat16
F32 = jnp.float32
MESH = pl.DeviceIdType.MESH
EPS = 1e-05

D = 14848
TOK = 128
KVW = 1024
N = 16
SH = D // N
RA = 480
RB = SH - RA
HALF = {0: RA // 2, 1: RB // 2}
BASE = {0: 0, 1: RA}
SIZE = {0: RA, 1: RB}


def div(a, b):
    return lax.div(a, jnp.int32(b))


def rem(a, b):
    return lax.rem(a, jnp.int32(b))


def kernel(x, cot, w, gain, bias, out, gw, gb,
           xT, tok, cots, stat, stats, hid, ghs, ghT, s_a, s_b, xr_a, xr_b,
           zs_a, zs_b, zr_a, zr_b, fin_a, fin_b, gcol, bcol, acc, gg, ggs, gtot,
           c_s, c_r, ta_s, ta_r, tb_s, tb_r, st_s, st_r, h_s, h_r,
           x_s, x_r, za_s, za_r, zb_s, zb_r, fa_s, fa_r, fb_s, fb_r, g_s, g_r, t_s, t_r, l_s):
    r = lax.axis_index("replica")
    o = lax.axis_index("outer")
    xlo, z = div(r, 8), rem(r, 8)
    xhi, y, c = div(o, 8), rem(div(o, 2), 4), rem(o, 2)

    def member(k, sign):
        dxh, dy, dc = div(k, 8), rem(div(k, 2), 4), rem(k, 2)
        xh = rem(xhi + dxh, 2)
        yy = rem(y + 4 + sign * dy, 4)
        cc = rem(c + dc, 2)
        xl = rem(xlo + dxh, 2)
        return xl * 8 + z, xh * 8 + yy * 2 + cc

    def ahead(k):
        return member(k, 1)

    def behind(k):
        return member(k, -1)

    def replica(k, sign):
        return rem(xlo + div(k, 8), 2) * 8 + rem(z + 8 + sign * rem(k, 8), 8), o

    bar = pltpu.get_barrier_semaphore()

    @pl.loop(1, N)
    def _(k):
        pl.semaphore_signal(bar, inc=1, device_id=ahead(k), device_id_type=MESH)
        pl.semaphore_signal(bar, inc=1, device_id=replica(k, 1), device_id_type=MESH)

    pl.semaphore_wait(bar, 2 * (N - 1))

    def remote(src, dst, ss, rs, dev):
        return pltpu.make_async_remote_copy(
            src_ref=src, dst_ref=dst, send_sem=ss, recv_sem=rs, device_id=dev, device_id_type=MESH)

    def rows(k, n=TOK):
        return pl.ds(pl.multiple_of(k * n, n), n)

    def cot_copy(k):
        return remote(cot, cots.at[rows(k)], c_s.at[k], c_r.at[k], ahead(k))

    def cot_forward(k):
        return remote(cots.at[rows(k)], cots.at[rows(k + 1)], c_s.at[k + 1], c_r.at[k + 1], ahead(jnp.int32(1)))

    own_cot = pltpu.make_async_copy(cot, cots.at[pl.ds(0, TOK)], l_s.at[0])
    own_cot.start()
    cot_copy(jnp.int32(1)).start()

    @pl.loop(1, 8)
    def _(j):
        cot_copy(2 * j).start()

    def turn(t, total):
        s = pl.multiple_of(t * 512, 512)
        v = x[:, pl.ds(s, 512)].T
        xT[pl.ds(s, 512), :] = v
        return total + v.astype(F32).reshape(64, 8, TOK).sum(0)

    total = lax.fori_loop(0, D // 512, turn, jnp.zeros((8, TOK), F32))
    mean = total.sum(0, keepdims=True) / D

    def tok_copy(k, part):
        ss, rs = (ta_s, ta_r) if part == 0 else (tb_s, tb_r)
        dev = ahead(k)
        at = pl.multiple_of(dev[1] * SH + BASE[part], 16)
        return remote(xT.at[pl.ds(at, SIZE[part])], tok.at[k, pl.ds(BASE[part], SIZE[part])],
                      ss.at[k], rs.at[k], dev)

    own_tok = pltpu.make_async_copy(xT.at[rows(o, SH)], tok.at[0], l_s.at[1])
    own_tok.start()
    for part in (0, 1):
        @pl.loop(1, N)
        def _(k):
            tok_copy(k, part).start()

    def spread(t, total):
        s = pl.multiple_of(t * 512, 512)
        v = xT[pl.ds(s, 512), :].astype(F32) - mean
        return total + (v * v).reshape(64, 8, TOK).sum(0)

    total = lax.fori_loop(0, D // 512, spread, jnp.zeros((8, TOK), F32))
    inv = lax.rsqrt(total.sum(0, keepdims=True) / D + EPS)
    stat[0:1, :] = mean
    stat[1:2, :] = inv
    stats[0, 0:1, :] = mean
    stats[0, 1:2, :] = inv

    def stat_copy(k):
        return remote(stat, stats.at[k], st_s.at[k], st_r.at[k], ahead(k))

    @pl.loop(1, N)
    def _(k):
        stat_copy(k).start()

    first_tile = pl.multiple_of(div(o * SH, 128) * 128, 128)
    shift = pl.multiple_of(rem(o, 4) * 32, 32)
    gcol[...] = jnp.broadcast_to(gain[:, pl.ds(first_tile, 1024)], (TOK, 1024)).T
    bcol[...] = jnp.broadcast_to(bias[:, pl.ds(first_tile, 1024)], (TOK, 1024)).T

    @pl.loop(1, 8)
    def _(j):
        cot_copy(2 * j).wait_recv()
        cot_forward(2 * j).start()

    own_cot.wait()

    @pl.loop(0, 8)
    def _(j):
        @pl.when(j == 0)
        def _():
            cot_copy(jnp.int32(1)).wait_recv()

        @pl.when(j > 0)
        def _():
            cot_forward(2 * j).wait_recv()

        v = lax.dot_general(w[...], cots[rows(j, 2 * TOK), :], (((1,), (1,)), ((), ())),
                            preferred_element_type=F32).astype(BF)
        ghs[2 * j] = v[:, :TOK]
        ghs[2 * j + 1] = v[:, TOK:]

    own_tok.wait()
    acc[...] = jnp.zeros_like(acc)

    def gh_copy(k):
        return remote(ghs.at[k], ghT.at[rows(o, SH)], h_s.at[k], h_r.at[k], behind(k))

    other = (rem(xlo + 1, 2) * 8 + z, o)

    def half_copy(part):
        s, xr = (s_a, xr_a) if part == 0 else (s_b, xr_b)
        h = HALF[part]
        return remote(s.at[:, pl.ds(pl.multiple_of((1 - xlo) * h, 16), h)], xr, x_s.at[part], x_r.at[part], other)

    for part in (0, 1):
        base, size = BASE[part], SIZE[part]
        s = (s_a, s_b)[part]

        @pl.loop(0, N)
        def _(k):
            @pl.when(k > 0)
            def _():
                tok_copy(k, part).wait_recv()
                if part == 0:
                    stat_copy(k).wait_recv()
            v = tok[k, base:base + size, :].astype(F32)
            normed = (v - stats[k, 0:1, :]) * stats[k, 1:2, :]
            at = pl.multiple_of(shift + base, 32)
            hid[0:size, rows(k)] = (gcol[pl.ds(at, size), :] * normed + bcol[pl.ds(at, size), :]).astype(BF)
            gh = ghs[k, base:base + size, :].astype(F32)
            acc[0, base:base + size, :] += gh * normed
            acc[1, base:base + size, :] += gh

        @pl.loop(0, 4)
        def _(n):
            v = jnp.dot(hid[0:size, :], cots[:, rows(n, 256)], preferred_element_type=F32).astype(BF)
            s[2 * n] = v[:, :128]
            s[2 * n + 1] = v[:, 128:]

        half_copy(part).start()
        if part == 0:
            own_gh = pltpu.make_async_copy(ghs.at[0], ghT.at[rows(o, SH)], l_s.at[2])
            own_gh.start()

            @pl.loop(1, N)
            def _(k):
                gh_copy(k).start()

    for i in (0, 1):
        for t in range(8):
            n = min(128, SH - t * 128)
            v = acc[i, t * 128:t * 128 + n, :].T.sum(0, keepdims=True)
            gg[i * 8 + t:i * 8 + t + 1, 0:n] = v
            if n < 128:
                gg[i * 8 + t:i * 8 + t + 1, n:128] = jnp.zeros((1, 128 - n), F32)

    def gg_copy(k):
        return remote(gg, ggs.at[r], g_s.at[k], g_r.at[k], replica(k, 1))

    ggs[r] = gg[...]

    @pl.loop(1, N)
    def _(k):
        gg_copy(k).start()

    def z_copy(part, k):
        zs, zr, ss, rs = ((zs_a, zr_a, za_s, za_r), (zs_b, zr_b, zb_s, zb_r))[part]
        dev = replica(k, 1)
        return remote(zs.at[rem(z + k, 8)], zr.at[k], ss.at[k], rs.at[k], dev)

    for part in (0, 1):
        s, xr, zs, zr = ((s_a, xr_a, zs_a, zr_a), (s_b, xr_b, zs_b, zr_b))[part]
        h = HALF[part]
        half_copy(part).wait_recv()
        mine = pl.multiple_of(xlo * h, 16)
        zs[...] = (s[:, pl.ds(mine, h), :].astype(F32) + xr[...].astype(F32)).astype(BF)

        @pl.loop(1, 8)
        def _(k):
            z_copy(part, k).start()

    def fin_copy(part, k):
        fin, ss, rs = ((fin_a, fa_s, fa_r), (fin_b, fb_s, fb_r))[part]
        h = HALF[part]
        at = pl.multiple_of(BASE[part] + xlo * h, 16)
        return remote(fin, gw.at[pl.ds(at, h), rows(z)], ss.at[k], rs.at[k], replica(k, 1))

    @pl.loop(1, N)
    def _(k):
        gg_copy(k).wait_recv()

    gtot[...] = ggs[...].sum(0) / N
    gb[o] = gtot[...]

    def gt_copy(k):
        return remote(gtot, gb.at[o], t_s.at[k], t_r.at[k], ahead(k))

    @pl.loop(1, N)
    def _(k):
        gt_copy(k).start()

    for part in (0, 1):
        s, xr, zs, zr, fin = ((s_a, xr_a, zs_a, zr_a, fin_a), (s_b, xr_b, zs_b, zr_b, fin_b))[part]
        h = HALF[part]

        @pl.loop(1, 8)
        def _(k):
            z_copy(part, k).wait_recv()

        mine = pl.multiple_of(xlo * h, 16)
        v = s[z, pl.ds(mine, h), :].astype(F32) + xr[z].astype(F32)
        for k in range(1, 8):
            v = v + zr[k].astype(F32)
        fin[...] = (v / N).astype(BF)
        gw[pl.ds(pl.multiple_of(BASE[part] + mine, 16), h), rows(z)] = fin[...]

        @pl.loop(1, N)
        def _(k):
            fin_copy(part, k).start()

    stat_t = jnp.broadcast_to(stat[0:1, :], (TOK, TOK)).T
    inv_t = jnp.broadcast_to(stat[1:2, :], (TOK, TOK)).T
    own_gh.wait()

    def piece(s, n, sums):
        g = ghT[pl.ds(s, n), :].T
        out[:, pl.ds(s, n)] = g
        a, b = sums
        for t in range(n // 128):
            at = pl.multiple_of(s + t * 128, 128)
            scaled = g[:, t * 128:t * 128 + 128].astype(F32) * gain[:, pl.ds(at, 128)]
            normed = (x[:, pl.ds(at, 128)].astype(F32) - stat_t) * inv_t
            a = a + scaled
            b = b + scaled * normed
        return a, b

    quarter = 2 * xhi + div(y, 2)
    sums = (jnp.zeros((TOK, TOK), F32), jnp.zeros((TOK, TOK), F32))

    def quarter_step(q, sums):
        qq = rem(quarter + q, 4)
        for m in range(4):
            po = qq * 4 + m
            pxh, py, pc = div(po, 8), rem(div(po, 2), 4), rem(po, 2)
            k = rem(pxh + xhi, 2) * 8 + rem(py + 4 - y, 4) * 2 + rem(pc + c, 2)

            @pl.when(k > 0)
            def _():
                gh_copy(k).wait_recv()

        start = qq * 3712

        def inner(t, sums):
            return piece(pl.multiple_of(start + t * 512, 128), 512, sums)

        sums = lax.fori_loop(0, 7, inner, sums)
        return piece(pl.multiple_of(start + 3584, 128), 128, sums)

    sums = lax.fori_loop(0, 4, quarter_step, sums)
    first = jnp.broadcast_to(sums[0].sum(1, keepdims=True) / D, (TOK, TOK))
    second = jnp.broadcast_to(sums[1].sum(1, keepdims=True) / D, (TOK, TOK))

    @pl.loop(0, D // 512)
    def _(t):
        for u in range(4):
            at = pl.multiple_of(t * 512 + u * 128, 128)
            scaled = out[:, pl.ds(at, 128)].astype(F32) * gain[:, pl.ds(at, 128)]
            normed = (x[:, pl.ds(at, 128)].astype(F32) - stat_t) * inv_t
            out[:, pl.ds(at, 128)] = (inv_t * (scaled - first - normed * second)).astype(BF)

    @pl.loop(1, N)
    def _(k):
        fin_copy(0, k).wait_recv()
        fin_copy(1, k).wait_recv()
        gt_copy(k).wait_recv()

    @pl.loop(1, N)
    def _(k):
        tok_copy(k, 0).wait_send()
        tok_copy(k, 1).wait_send()
        stat_copy(k).wait_send()
        gh_copy(k).wait_send()
        gg_copy(k).wait_send()
        gt_copy(k).wait_send()
        fin_copy(0, k).wait_send()
        fin_copy(1, k).wait_send()

    cot_copy(jnp.int32(1)).wait_send()

    @pl.loop(1, 8)
    def _(j):
        cot_copy(2 * j).wait_send()
        cot_forward(2 * j).wait_send()
        z_copy(0, j).wait_send()
        z_copy(1, j).wait_send()

    half_copy(0).wait_send()
    half_copy(1).wait_send()


def body(tokens, cotangent, kv_weight, gain, bias):
    V = pl.BlockSpec(memory_space=pltpu.VMEM)
    ha, hb = HALF[0], HALF[1]
    scratch = [
        pltpu.VMEM((D, TOK), BF),
        pltpu.VMEM((N, SH, TOK), BF),
        pltpu.VMEM((N * TOK, KVW), BF),
        pltpu.VMEM((8, TOK), F32),
        pltpu.VMEM((N, 8, TOK), F32),
        pltpu.VMEM((RA, N * TOK), BF),
        pltpu.VMEM((N, SH, TOK), BF),
        pltpu.VMEM((D, TOK), BF),
        pltpu.VMEM((8, RA, 128), BF),
        pltpu.VMEM((8, RB, 128), BF),
        pltpu.VMEM((8, ha, 128), BF),
        pltpu.VMEM((8, hb, 128), BF),
        pltpu.VMEM((8, ha, 128), BF),
        pltpu.VMEM((8, hb, 128), BF),
        pltpu.VMEM((8, ha, 128), BF),
        pltpu.VMEM((8, hb, 128), BF),
        pltpu.VMEM((ha, 128), BF),
        pltpu.VMEM((hb, 128), BF),
        pltpu.VMEM((1024, TOK), F32),
        pltpu.VMEM((1024, TOK), F32),
        pltpu.VMEM((2, SH, TOK), F32),
        pltpu.VMEM((N, 128), F32),
        pltpu.VMEM((N, N, 128), F32),
        pltpu.VMEM((N, 128), F32),
    ]
    dma = pltpu.SemaphoreType.DMA
    sems = [dma((N,))] * 10 + [dma((2,))] * 2 + [dma((8,))] * 4 + [dma((N,))] * 8 + [dma((3,))]
    out, gw, gb = pl.pallas_call(
        kernel,
        out_shape=(
            jax.ShapeDtypeStruct((TOK, D), BF),
            jax.ShapeDtypeStruct((SH, KVW), BF),
            jax.ShapeDtypeStruct((N, N, 128), F32),
        ),
        in_specs=[V] * 5,
        out_specs=(V, V, V),
        scratch_shapes=scratch + sems,
        compiler_params=pltpu.CompilerParams(
            collective_id=0, has_side_effects=True, vmem_limit_bytes=60 << 20),
    )(tokens, cotangent, kv_weight, gain.reshape(1, D), bias.reshape(1, D))
    gb = gb.reshape(N, 2, 1024)[:, :, :SH]
    return out, gw, gb[:, 0].reshape(D), gb[:, 1].reshape(D)


def solution(mesh):
    in_specs = (
        P(("replica", "outer"), None),
        P(("replica", "outer"), None),
        P("outer", None),
        P(),
        P(),
    )
    out_specs = (P(("replica", "outer"), None), P("outer", None), P(), P())
    return jax.shard_map(body, mesh=mesh, in_specs=in_specs, out_specs=out_specs, check_vma=False)
```

```python
import jax
import jax.numpy as jnp
from jax import lax
from jax.experimental import pallas as pl
from jax.experimental.pallas import tpu as pltpu
from jax.sharding import PartitionSpec as P

BF = jnp.bfloat16
F32 = jnp.float32
MESH = pl.DeviceIdType.MESH
EPS = 1e-05

D = 14848
TOK = 128
KVW = 1024
COLS = 3712
AHEAD = 2
GH_AT = 2
N = 16
SH = D // N
BASE = (0, 256, 480, 704)
SIZE = (256, 224, 224, 224)
HBASE = (0, 128, 240, 352)
HALF = (128, 112, 112, 112)
NP = 4


def div(a, b):
    return lax.div(a, jnp.int32(b))


def rem(a, b):
    return lax.rem(a, jnp.int32(b))


def kernel(x, cot, w, gain, bias, gh_out, gw, gb, sums_out,
           xT, tok, cots, stat, stats, hid, ghs, ghT, s_buf, xr, zs, zr, fin,
           gcol, bcol, acc, gg, ggs, gtot,
           c_s, c_r, tk_s, tk_r, st_s, st_r, h_s, h_r, x_s, x_r, z_s, z_r, f_s, f_r, p_s, p_r,
           g_s, g_r, t_s, t_r, l_s):
    r = lax.axis_index("replica")
    o = lax.axis_index("outer")
    xlo, z = div(r, 8), rem(r, 8)
    xhi, y, c = div(o, 8), rem(div(o, 2), 4), rem(o, 2)

    def member(k, sign):
        dxh, dy, dc = div(k, 8), rem(div(k, 2), 4), rem(k, 2)
        xh = rem(xhi + dxh, 2)
        yy = rem(y + 4 + sign * dy, 4)
        cc = rem(c + dc, 2)
        xl = rem(xlo + dxh, 2)
        return xl * 8 + z, xh * 8 + yy * 2 + cc

    def ahead(k):
        return member(k, 1)

    def behind(k):
        return member(k, -1)

    def replica(k, sign):
        return rem(xlo + div(k, 8), 2) * 8 + rem(z + 8 + sign * rem(k, 8), 8), o

    bar = pltpu.get_barrier_semaphore()

    @pl.loop(1, N)
    def _(k):
        pl.semaphore_signal(bar, inc=1, device_id=ahead(k), device_id_type=MESH)
        pl.semaphore_signal(bar, inc=1, device_id=replica(k, 1), device_id_type=MESH)

    pl.semaphore_wait(bar, 2 * (N - 1))

    def remote(src, dst, ss, rs, dev):
        return pltpu.make_async_remote_copy(
            src_ref=src, dst_ref=dst, send_sem=ss, recv_sem=rs, device_id=dev, device_id_type=MESH)

    def rows(k, n=TOK):
        return pl.ds(pl.multiple_of(k * n, n), n)

    def cot_copy(k):
        return remote(cot, cots.at[rows(k)], c_s.at[k], c_r.at[k], ahead(k))

    def cot_forward(k):
        return remote(cots.at[rows(k)], cots.at[rows(k + 1)], c_s.at[k + 1], c_r.at[k + 1], ahead(jnp.int32(1)))

    own_cot = pltpu.make_async_copy(cot, cots.at[pl.ds(0, TOK)], l_s.at[0])
    own_cot.start()
    cot_copy(jnp.int32(1)).start()

    @pl.loop(1, 8)
    def _(j):
        cot_copy(2 * j).start()

    def turn(t, total):
        s = pl.multiple_of(t * 512, 512)
        v = x[:, pl.ds(s, 512)].T
        xT[pl.ds(s, 512), :] = v
        return total + v.astype(F32).reshape(64, 8, TOK).sum(0)

    total = lax.fori_loop(0, D // 512, turn, jnp.zeros((8, TOK), F32))
    mean = total.sum(0, keepdims=True) / D

    def tok_copy(k, part):
        dev = ahead(k)
        at = pl.multiple_of(dev[1] * SH + BASE[part], 16)
        return remote(xT.at[pl.ds(at, SIZE[part])], tok.at[k, pl.ds(BASE[part], SIZE[part])],
                      tk_s.at[part, k], tk_r.at[part, k], dev)

    own_tok = pltpu.make_async_copy(xT.at[rows(o, SH)], tok.at[0], l_s.at[1])
    own_tok.start()
    def tok_start(part):
        @pl.loop(1, N)
        def _(k):
            tok_copy(k, part).start()

    for part in range(AHEAD):
        tok_start(part)

    def spread(t, total):
        s = pl.multiple_of(t * 512, 512)
        v = xT[pl.ds(s, 512), :].astype(F32) - mean
        return total + (v * v).reshape(64, 8, TOK).sum(0)

    total = lax.fori_loop(0, D // 512, spread, jnp.zeros((8, TOK), F32))
    inv = lax.rsqrt(total.sum(0, keepdims=True) / D + EPS)
    stat[0:1, :] = mean
    stat[1:2, :] = inv
    stats[0, 0:1, :] = mean
    stats[0, 1:2, :] = inv

    def stat_copy(k):
        return remote(stat, stats.at[k], st_s.at[k], st_r.at[k], ahead(k))

    @pl.loop(1, N)
    def _(k):
        stat_copy(k).start()

    first_tile = div(o * SH, 128)
    shift = pl.multiple_of(rem(o, 4) * 32, 32)
    for t in range(8):
        gcol[t * 128:t * 128 + 128, :] = jnp.broadcast_to(gain[pl.ds(first_tile + t, 1), :], (TOK, 128)).T
        bcol[t * 128:t * 128 + 128, :] = jnp.broadcast_to(bias[pl.ds(first_tile + t, 1), :], (TOK, 128)).T

    @pl.loop(1, 8)
    def _(j):
        cot_copy(2 * j).wait_recv()
        cot_forward(2 * j).start()

    own_cot.wait()

    @pl.loop(0, 8)
    def _(j):
        @pl.when(j == 0)
        def _():
            cot_copy(jnp.int32(1)).wait_recv()

        @pl.when(j > 0)
        def _():
            cot_forward(2 * j).wait_recv()

        v = lax.dot_general(w[...], cots[rows(j, 2 * TOK), :], (((1,), (1,)), ((), ())),
                            preferred_element_type=F32).astype(BF)
        ghs[2 * j] = v[:, :TOK]
        ghs[2 * j + 1] = v[:, TOK:]

    own_tok.wait()
    acc[...] = jnp.zeros_like(acc)

    def gh_copy(k):
        return remote(ghs.at[k], ghT.at[rows(o, SH)], h_s.at[k], h_r.at[k], behind(k))

    own_gh = pltpu.make_async_copy(ghs.at[0], ghT.at[rows(o, SH)], l_s.at[2])
    own_gh.start()

    beside = replica(jnp.int32(8), 1)

    def half_copy(part):
        h = HALF[part]
        at = pl.multiple_of(BASE[part] + (1 - xlo) * h, 16)
        return remote(s_buf.at[:, pl.ds(at, h)], xr.at[:, pl.ds(HBASE[part], h)], x_s.at[part], x_r.at[part], beside)

    def z_copy(part, k):
        at = pl.ds(HBASE[part], HALF[part])
        return remote(zs.at[rem(z + k, 8), at], zr.at[k, at], z_s.at[part, k], z_r.at[part, k], replica(k, 1))

    def gw_at(part, zz):
        return gw.at[pl.ds(pl.multiple_of(BASE[part] + xlo * HALF[part], 16), HALF[part]), rows(zz)]

    def fin_copy(part, k):
        return remote(fin.at[pl.ds(HBASE[part], HALF[part])], gw_at(part, z), f_s.at[part, k], f_r.at[part, k],
                      replica(k, 1))

    def pass_copy(part, k):
        here = gw_at(part, rem(z + 8 - k, 8))
        return remote(here, here, p_s.at[part, k], p_r.at[part, k], beside)

    def weight_part(part):
        base, size = BASE[part], SIZE[part]

        @pl.loop(1, N)
        def _(k):
            tok_copy(k, part).wait_recv()
            if part == 0:
                stat_copy(k).wait_recv()

        if part + AHEAD < NP:
            tok_start(part + AHEAD)

        step = size // 2
        for u in range(2):
            lo = base + u * step

            def block(k, carry):
                ag, ab = carry
                normed = (tok[k, lo:lo + step, :].astype(F32) - stats[k, 0:1, :]) * stats[k, 1:2, :]
                at = pl.multiple_of(shift + lo, 16)
                hid[u * step:(u + 1) * step, rows(k)] = (
                    gcol[pl.ds(at, step), :] * normed + bcol[pl.ds(at, step), :]).astype(BF)
                gh = ghs[k, lo:lo + step, :].astype(F32)
                return ag + gh * normed, ab + gh

            zero = jnp.zeros((step, TOK), F32)
            ag, ab = lax.fori_loop(0, N, block, (zero, zero))
            at = pl.multiple_of(shift + lo, 16)
            acc[0, pl.ds(at, step), :] = ag
            acc[1, pl.ds(at, step), :] = ab

        @pl.loop(0, 4)
        def _(n):
            v = jnp.dot(hid[0:size, :], cots[:, rows(n, 256)], preferred_element_type=F32).astype(BF)
            s_buf[2 * n, base:base + size, :] = v[:, :128]
            s_buf[2 * n + 1, base:base + size, :] = v[:, 128:]

        half_copy(part).start()

    def beside_part(part):
        h, hb = HALF[part], HBASE[part]
        half_copy(part).wait_recv()
        at = pl.multiple_of(BASE[part] + xlo * h, 16)
        for n in range(8):
            zs[n, hb:hb + h, :] = (
                s_buf[n, pl.ds(at, h), :].astype(F32) + xr[n, hb:hb + h, :].astype(F32)).astype(BF)

        @pl.loop(1, 8)
        def _(k):
            z_copy(part, k).start()

    def own_part(part):
        h, hb = HALF[part], HBASE[part]

        @pl.loop(1, 8)
        def _(k):
            z_copy(part, k).wait_recv()

        at = pl.multiple_of(BASE[part] + xlo * h, 16)
        v = s_buf[z, pl.ds(at, h), :].astype(F32) + xr[z, hb:hb + h, :].astype(F32)
        for k in range(1, 8):
            v = v + zr[k, hb:hb + h, :].astype(F32)
        v = (v / N).astype(BF)
        fin[hb:hb + h, :] = v
        gw[pl.ds(at, h), rows(z)] = v

        @pl.loop(1, 8)
        def _(k):
            fin_copy(part, k).start()

        pass_copy(part, jnp.int32(0)).start()

    def pass_part(part):
        @pl.loop(1, 8)
        def _(k):
            fin_copy(part, k).wait_recv()
            pass_copy(part, k).start()

    def gg_copy(k):
        return remote(gg, ggs.at[r], g_s.at[k], g_r.at[k], replica(k, 1))

    def gt_copy(k):
        return remote(gtot, gb.at[o], t_s.at[k], t_r.at[k], ahead(k))

    for i in range(NP + 3):
        if i < NP:
            weight_part(i)
        if i == GH_AT:
            @pl.loop(1, N)
            def _(k):
                gh_copy(k).start()
        if i == NP - 1:
            for j in (0, 1):
                for t in range(8):
                    gg[j * 8 + t:j * 8 + t + 1, :] = acc[j, t * 128:t * 128 + 128, :].T.sum(0, keepdims=True)
            ggs[r] = gg[...]

            @pl.loop(1, N)
            def _(k):
                gg_copy(k).start()
        if 0 <= i - 1 < NP:
            beside_part(i - 1)
        if 0 <= i - 2 < NP:
            own_part(i - 2)
        if 0 <= i - 3 < NP:
            pass_part(i - 3)
        if i == NP:
            @pl.loop(1, N)
            def _(k):
                gg_copy(k).wait_recv()

            gtot[...] = ggs[...].sum(0) / N
            gb[o] = gtot[...]

            @pl.loop(1, N)
            def _(k):
                gt_copy(k).start()

    stat_t = jnp.broadcast_to(stat[0:1, :], (TOK, TOK)).T
    inv_t = jnp.broadcast_to(stat[1:2, :], (TOK, TOK)).T
    own_gh.wait()

    def piece(s, n, sums):
        g = ghT[pl.ds(s, n), :].T
        gh_out[:, pl.ds(s, n)] = g
        a, b = sums
        for t in range(n // 128):
            at = pl.multiple_of(s + t * 128, 128)
            scaled = g[:, t * 128:t * 128 + 128].astype(F32) * gain[pl.ds(div(s, 128) + t, 1), :]
            normed = (x[:, pl.ds(at, 128)].astype(F32) - stat_t) * inv_t
            a = a + scaled
            b = b + scaled * normed
        return a, b

    quarter = 2 * xhi + div(y, 2)
    sums = (jnp.zeros((TOK, TOK), F32), jnp.zeros((TOK, TOK), F32))

    def quarter_step(q, sums):
        qq = rem(quarter + q, 4)
        for m in range(4):
            po = qq * 4 + m
            pxh, py, pc = div(po, 8), rem(div(po, 2), 4), rem(po, 2)
            k = rem(pxh + xhi, 2) * 8 + rem(py + 4 - y, 4) * 2 + rem(pc + c, 2)

            @pl.when(k > 0)
            def _():
                gh_copy(k).wait_recv()

        start = qq * 3712

        def inner(t, sums):
            return piece(pl.multiple_of(start + t * 512, 128), 512, sums)

        sums = lax.fori_loop(0, 7, inner, sums)
        return piece(pl.multiple_of(start + 3584, 128), 128, sums)

    sums = lax.fori_loop(0, 4, quarter_step, sums)
    sums_out[0] = stat_t
    sums_out[1] = inv_t
    sums_out[2] = jnp.broadcast_to(sums[0].sum(1, keepdims=True) / D, (TOK, TOK))
    sums_out[3] = jnp.broadcast_to(sums[1].sum(1, keepdims=True) / D, (TOK, TOK))

    for part in range(NP):
        pass_copy(part, jnp.int32(0)).wait_recv()
        pass_copy(part, jnp.int32(0)).wait_send()
        half_copy(part).wait_send()

        @pl.loop(1, 8)
        def _(k):
            pass_copy(part, k).wait_recv()
            pass_copy(part, k).wait_send()
            fin_copy(part, k).wait_send()
            z_copy(part, k).wait_send()

        @pl.loop(1, N)
        def _(k):
            tok_copy(k, part).wait_send()

    @pl.loop(1, N)
    def _(k):
        gt_copy(k).wait_recv()
        stat_copy(k).wait_send()
        gh_copy(k).wait_send()
        gg_copy(k).wait_send()
        gt_copy(k).wait_send()

    cot_copy(jnp.int32(1)).wait_send()

    @pl.loop(1, 8)
    def _(j):
        cot_copy(2 * j).wait_send()
        cot_forward(2 * j).wait_send()


def finish(x, gh, gain, sums, gw, gb, out, gw_out, gg_out):
    t = pl.program_id(0)

    @pl.when(t == 0)
    def _():
        gw_out[...] = gw[...]
        gg_out[...] = jnp.zeros_like(gg_out)
        for j in (0, 1):
            for m in range(N):
                at = 29 * (m // 4) + 7 * (m % 4)
                gg_out[j, at:at + 8, :] += gb[m, 8 * j:8 * j + 8, :]

    for u in range(COLS // 128):
        at = slice(u * 128, u * 128 + 128)
        scaled = gh[:, at].astype(F32) * gain[pl.ds(t * (COLS // 128) + u, 1), :]
        normed = (x[:, at].astype(F32) - sums[0]) * sums[1]
        out[:, at] = (sums[1] * (scaled - sums[2] - normed * sums[3])).astype(BF)


def body(tokens, cotangent, kv_weight, gain, bias):
    V = pl.BlockSpec(memory_space=pltpu.VMEM)
    half = SH // 2
    scratch = [
        pltpu.VMEM((D, TOK), BF),
        pltpu.VMEM((N, SH, TOK), BF),
        pltpu.VMEM((N * TOK, KVW), BF),
        pltpu.VMEM((8, TOK), F32),
        pltpu.VMEM((N, 8, TOK), F32),
        pltpu.VMEM((max(SIZE), N * TOK), BF),
        pltpu.VMEM((N, SH, TOK), BF),
        pltpu.VMEM((D, TOK), BF),
        pltpu.VMEM((8, SH, 128), BF),
        pltpu.VMEM((8, half, 128), BF),
        pltpu.VMEM((8, half, 128), BF),
        pltpu.VMEM((8, half, 128), BF),
        pltpu.VMEM((half, 128), BF),
        pltpu.VMEM((1024, TOK), F32),
        pltpu.VMEM((1024, TOK), F32),
        pltpu.VMEM((2, 1024, TOK), F32),
        pltpu.VMEM((N, 128), F32),
        pltpu.VMEM((N, N, 128), F32),
        pltpu.VMEM((N, 128), F32),
    ]
    dma = pltpu.SemaphoreType.DMA
    sems = ([dma((N,))] * 2 + [dma((NP, N))] * 2 + [dma((N,))] * 4 + [dma((NP,))] * 2
            + [dma((NP, 8))] * 6 + [dma((N,))] * 4 + [dma((3,))])
    gain, bias = gain.reshape(D // 128, 128), bias.reshape(D // 128, 128)
    gh, gw, gb, sums = pl.pallas_call(
        kernel,
        out_shape=(
            jax.ShapeDtypeStruct((TOK, D), BF),
            jax.ShapeDtypeStruct((SH, KVW), BF),
            jax.ShapeDtypeStruct((N, N, 128), F32),
            jax.ShapeDtypeStruct((4, TOK, TOK), F32),
        ),
        in_specs=[V] * 5,
        out_specs=(V, V, V, V),
        scratch_shapes=scratch + sems,
        compiler_params=pltpu.CompilerParams(
            collective_id=0, has_side_effects=True, vmem_limit_bytes=60 << 20),
    )(tokens, cotangent, kv_weight, gain, bias)
    tile = pl.BlockSpec((TOK, COLS), lambda t: (0, t))
    out, gw, gg = pl.pallas_call(
        finish,
        grid=(D // COLS,),
        out_shape=(
            jax.ShapeDtypeStruct((TOK, D), BF),
            jax.ShapeDtypeStruct((SH, KVW), BF),
            jax.ShapeDtypeStruct((2, D // 128, 128), F32),
        ),
        in_specs=[tile, tile, V, V, V, V],
        out_specs=(tile, V, V),
        compiler_params=pltpu.CompilerParams(vmem_limit_bytes=60 << 20),
    )(tokens, gh, gain, sums, gw, gb)
    return out, gw, gg[0].reshape(D), gg[1].reshape(D)


def solution(mesh):
    in_specs = (
        P(("replica", "outer"), None),
        P(("replica", "outer"), None),
        P("outer", None),
        P(),
        P(),
    )
    out_specs = (P(("replica", "outer"), None), P("outer", None), P(), P())
    return jax.shard_map(body, mesh=mesh, in_specs=in_specs, out_specs=out_specs, check_vma=False)
```

```python
import jax
import jax.numpy as jnp
from jax import lax
from jax.experimental import pallas as pl
from jax.experimental.pallas import tpu as pltpu
from jax.sharding import PartitionSpec as P

BF = jnp.bfloat16
F32 = jnp.float32
MESH = pl.DeviceIdType.MESH
EPS = 1e-05

D = 14848
TOK = 128
KVW = 1024
COLS = 3712
AHEAD = 2
GH_AT = 3
N = 16
SH = D // N
BASE = (0, 192, 384, 576, 768)
SIZE = (192, 192, 192, 192, 160)
HBASE = (0, 96, 192, 288, 384)
HALF = (96, 96, 96, 96, 80)
NP = 5


def div(a, b):
    return lax.div(a, jnp.int32(b))


def rem(a, b):
    return lax.rem(a, jnp.int32(b))


def kernel(x_hbm, cot, w_hbm, gain, bias, ghT, gw, gb, sums_out,
           x, w, xT, tok, cots, stat, stats, hid, ghs, s_buf, xr, zs, zr, fin,
           gcol, bcol, acc, gg, ggs, gtot, tsum, tsums,
           c_s, c_r, e_s, e_r, tk_s, tk_r, st_s, st_r, h_s, h_r, x_s, x_r, z_s, z_r, f_s, f_r, p_s, p_r,
           g_s, g_r, t_s, t_r, u_s, u_r, l_s):
    r = lax.axis_index("replica")
    o = lax.axis_index("outer")
    xlo, z = div(r, 8), rem(r, 8)
    xhi, y, c = div(o, 8), rem(div(o, 2), 4), rem(o, 2)

    def member(k, sign):
        dxh, dy, dc = div(k, 8), rem(div(k, 2), 4), rem(k, 2)
        xh = rem(xhi + dxh, 2)
        yy = rem(y + 4 + sign * dy, 4)
        cc = rem(c + dc, 2)
        xl = rem(xlo + dxh, 2)
        return xl * 8 + z, xh * 8 + yy * 2 + cc

    def ahead(k):
        return member(k, 1)

    def behind(k):
        return member(k, -1)

    def replica(k, sign):
        return rem(xlo + div(k, 8), 2) * 8 + rem(z + 8 + sign * rem(k, 8), 8), o

    bar = pltpu.get_barrier_semaphore()

    @pl.loop(1, N)
    def _(k):
        pl.semaphore_signal(bar, inc=1, device_id=ahead(k), device_id_type=MESH)
        pl.semaphore_signal(bar, inc=1, device_id=replica(k, 1), device_id_type=MESH)

    def remote(src, dst, ss, rs, dev):
        return pltpu.make_async_remote_copy(
            src_ref=src, dst_ref=dst, send_sem=ss, recv_sem=rs, device_id=dev, device_id_type=MESH)

    def rows(k, n=TOK):
        return pl.ds(pl.multiple_of(k * n, n), n)

    x_in = pltpu.make_async_copy(x_hbm, x, l_s.at[3])
    x_in.start()
    w_in = pltpu.make_async_copy(w_hbm, w, l_s.at[4])
    w_in.start()

    def cot_copy(k):
        return remote(cot, cots.at[rows(k)], c_s.at[k], c_r.at[k], ahead(k))

    def cot_along_y(j):
        at = pl.multiple_of((8 + 2 * j) * TOK, TOK)
        return remote(cots.at[pl.ds(8 * TOK, TOK // 2)], cots.at[pl.ds(at, TOK // 2)],
                      c_s.at[8 + 2 * j], c_r.at[8 + 2 * j], ahead(2 * j))

    def cot_along_x(j):
        at = pl.multiple_of((8 + 2 * j) * TOK + TOK // 2, TOK // 2)
        here = pl.multiple_of(2 * j * TOK + TOK // 2, TOK // 2)
        return remote(cots.at[pl.ds(here, TOK // 2)], cots.at[pl.ds(at, TOK // 2)],
                      e_s.at[j], e_r.at[j], ahead(jnp.int32(8)))

    def cot_forward(k):
        return remote(cots.at[rows(k)], cots.at[rows(k + 1)], c_s.at[k + 1], c_r.at[k + 1], ahead(jnp.int32(1)))

    own_cot = pltpu.make_async_copy(cot, cots.at[pl.ds(0, TOK)], l_s.at[0])
    own_cot.start()

    x_in.wait()

    def turn(t, total):
        s = pl.multiple_of(t * 512, 512)
        v = x[:, pl.ds(s, 512)].T
        xT[pl.ds(s, 512), :] = v
        return total + v.astype(F32).reshape(64, 8, TOK).sum(0)

    total = lax.fori_loop(0, D // 512, turn, jnp.zeros((8, TOK), F32))
    mean = total.sum(0, keepdims=True) / D

    pl.semaphore_wait(bar, 2 * (N - 1))
    cot_copy(jnp.int32(8)).start()
    cot_copy(jnp.int32(1)).start()

    @pl.loop(1, 4)
    def _(j):
        cot_copy(2 * j).start()

    def tok_copy(k, part):
        dev = ahead(k)
        at = pl.multiple_of(dev[1] * SH + BASE[part], 16)
        return remote(xT.at[pl.ds(at, SIZE[part])], tok.at[k, pl.ds(BASE[part], SIZE[part])],
                      tk_s.at[part, k], tk_r.at[part, k], dev)

    own_tok = pltpu.make_async_copy(xT.at[rows(o, SH)], tok.at[0], l_s.at[1])
    own_tok.start()
    def tok_start(part):
        @pl.loop(1, N)
        def _(k):
            tok_copy(k, part).start()

    for part in range(AHEAD):
        tok_start(part)

    def spread(t, total):
        s = pl.multiple_of(t * 512, 512)
        v = xT[pl.ds(s, 512), :].astype(F32) - mean
        return total + (v * v).reshape(64, 8, TOK).sum(0)

    total = lax.fori_loop(0, D // 512, spread, jnp.zeros((8, TOK), F32))
    inv = lax.rsqrt(total.sum(0, keepdims=True) / D + EPS)
    stat[0:1, :] = mean
    stat[1:2, :] = inv
    stats[0, 0:1, :] = mean
    stats[0, 1:2, :] = inv

    def stat_copy(k):
        return remote(stat, stats.at[k], st_s.at[k], st_r.at[k], ahead(k))

    @pl.loop(1, N)
    def _(k):
        stat_copy(k).start()

    first_tile = div(o * SH, 128)
    shift = pl.multiple_of(rem(o, 4) * 32, 32)
    for t in range(8):
        gcol[t * 128:t * 128 + 128, :] = jnp.broadcast_to(gain[pl.ds(first_tile + t, 1), :], (TOK, 128)).T
        bcol[t * 128:t * 128 + 128, :] = jnp.broadcast_to(bias[pl.ds(first_tile + t, 1), :], (TOK, 128)).T

    cot_copy(jnp.int32(8)).wait_recv()

    @pl.loop(1, 4)
    def _(j):
        cot_along_y(j).start()

    cot_forward(jnp.int32(8)).start()

    @pl.loop(1, 4)
    def _(j):
        cot_copy(2 * j).wait_recv()
        cot_along_x(j).start()
        cot_forward(2 * j).start()

    @pl.loop(1, 4)
    def _(j):
        cot_along_y(j).wait_recv()
        cot_along_x(j).wait_recv()
        cot_forward(8 + 2 * j).start()

    own_cot.wait()
    w_in.wait()
    tsum[...] = jnp.zeros_like(tsum)

    own_tok.wait()
    acc[...] = jnp.zeros_like(acc)

    def gh_copy(k):
        return remote(ghs.at[k], ghT.at[rows(o, SH)], h_s.at[k], h_r.at[k], behind(k))

    beside = replica(jnp.int32(8), 1)

    def half_copy(part):
        h = HALF[part]
        at = pl.multiple_of(BASE[part] + (1 - xlo) * h, 16)
        return remote(s_buf.at[:, pl.ds(at, h)], xr.at[:, pl.ds(HBASE[part], h)], x_s.at[part], x_r.at[part], beside)

    def z_copy(part, k):
        at = pl.ds(HBASE[part], HALF[part])
        return remote(zs.at[rem(z + k, 8), at], zr.at[k, at], z_s.at[part, k], z_r.at[part, k], replica(k, 1))

    def gw_at(part, zz):
        return gw.at[pl.ds(pl.multiple_of(BASE[part] + xlo * HALF[part], 16), HALF[part]), rows(zz)]

    def fin_copy(part, k):
        return remote(fin.at[pl.ds(HBASE[part], HALF[part])], gw_at(part, z), f_s.at[part, k], f_r.at[part, k],
                      replica(k, 1))

    def pass_copy(part, k):
        here = gw_at(part, rem(z + 8 - k, 8))
        return remote(here, here, p_s.at[part, k], p_r.at[part, k], beside)

    def receive_part(part):
        @pl.loop(1, N)
        def _(k):
            tok_copy(k, part).wait_recv()
            if part == 0:
                stat_copy(k).wait_recv()
            if part + AHEAD < NP:
                tok_copy(k, part + AHEAD).start()
            if part == GH_AT:
                gh_copy(k).start()

    def weight_part(part):
        base, size = BASE[part], SIZE[part]

        step = size // 2
        for u in range(2):
            lo = base + u * step

            def block(k, carry):
                ag, ab = carry
                normed = (tok[k, lo:lo + step, :].astype(F32) - stats[k, 0:1, :]) * stats[k, 1:2, :]
                at = pl.multiple_of(shift + lo, 16)
                hid[u * step:(u + 1) * step, rows(k)] = (
                    gcol[pl.ds(at, step), :] * normed + bcol[pl.ds(at, step), :]).astype(BF)
                gh = ghs[k, lo:lo + step, :].astype(F32)
                scaled = gcol[pl.ds(at, step), :] * gh
                tsum[k, 0:8, :] += scaled.reshape(step // 8, 8, TOK).sum(0)
                tsum[k, 8:16, :] += (scaled * normed).reshape(step // 8, 8, TOK).sum(0)
                return ag + gh * normed, ab + gh

            zero = jnp.zeros((step, TOK), F32)
            ag, ab = lax.fori_loop(0, N, block, (zero, zero))
            at = pl.multiple_of(shift + lo, 16)
            acc[0, pl.ds(at, step), :] = ag
            acc[1, pl.ds(at, step), :] = ab

        @pl.loop(0, 4)
        def _(n):
            v = jnp.dot(hid[0:size, :], cots[:, rows(n, 256)], preferred_element_type=F32).astype(BF)
            s_buf[2 * n, base:base + size, :] = v[:, :128]
            s_buf[2 * n + 1, base:base + size, :] = v[:, 128:]

        half_copy(part).start()

    def beside_part(part):
        h, hb = HALF[part], HBASE[part]
        half_copy(part).wait_recv()
        at = pl.multiple_of(BASE[part] + xlo * h, 16)
        for n in range(8):
            zs[n, hb:hb + h, :] = (
                s_buf[n, pl.ds(at, h), :].astype(F32) + xr[n, hb:hb + h, :].astype(F32)).astype(BF)

        @pl.loop(1, 8)
        def _(k):
            z_copy(part, k).start()

    def own_part(part):
        h, hb = HALF[part], HBASE[part]

        @pl.loop(1, 8)
        def _(k):
            z_copy(part, k).wait_recv()

        at = pl.multiple_of(BASE[part] + xlo * h, 16)
        v = s_buf[z, pl.ds(at, h), :].astype(F32) + xr[z, hb:hb + h, :].astype(F32)
        for k in range(1, 8):
            v = v + zr[k, hb:hb + h, :].astype(F32)
        v = (v / N).astype(BF)
        fin[hb:hb + h, :] = v
        gw[pl.ds(at, h), rows(z)] = v

        @pl.loop(1, 8)
        def _(k):
            fin_copy(part, k).start()

        pass_copy(part, jnp.int32(0)).start()

    def pass_part(part):
        @pl.loop(1, 8)
        def _(k):
            fin_copy(part, k).wait_recv()
            pass_copy(part, k).start()

    def gg_copy(k):
        return remote(gg, ggs.at[r], g_s.at[k], g_r.at[k], replica(k, 1))

    def sum_copy(k):
        return remote(tsum.at[k], tsums.at[k], u_s.at[k], u_r.at[k], behind(k))

    def gt_copy(k):
        return remote(gtot, gb.at[o], t_s.at[k], t_r.at[k], ahead(k))

    receive_part(0)

    @pl.loop(0, 8)
    def _(j):
        @pl.when(j == 0)
        def _():
            cot_copy(jnp.int32(1)).wait_recv()

        @pl.when(j > 0)
        def _():
            cot_forward(2 * j).wait_recv()

        v = lax.dot_general(w[...], cots[rows(j, 2 * TOK), :], (((1,), (1,)), ((), ())),
                            preferred_element_type=F32).astype(BF)
        ghs[2 * j] = v[:, :TOK]
        ghs[2 * j + 1] = v[:, TOK:]

    own_gh = pltpu.make_async_copy(ghs.at[0], ghT.at[rows(o, SH)], l_s.at[2])
    own_gh.start()

    for i in range(NP + 3):
        if i < NP:
            if i > 0:
                receive_part(i)
            weight_part(i)
        if i == NP - 1:
            for j in (0, 1):
                for t in range(8):
                    gg[j * 8 + t:j * 8 + t + 1, :] = acc[j, t * 128:t * 128 + 128, :].T.sum(0, keepdims=True)
            ggs[r] = gg[...]

            @pl.loop(1, N)
            def _(k):
                sum_copy(k).start()
                gg_copy(k).start()
        if 0 <= i - 1 < NP:
            beside_part(i - 1)
        if 0 <= i - 2 < NP:
            own_part(i - 2)
        if 0 <= i - 3 < NP:
            pass_part(i - 3)
        if i == NP:
            @pl.loop(1, N)
            def _(k):
                gg_copy(k).wait_recv()

            gtot[...] = ggs[...].sum(0) / N
            gb[o] = gtot[...]

            @pl.loop(1, N)
            def _(k):
                gt_copy(k).start()

    total = tsum[0]
    for k in range(1, N):
        sum_copy(jnp.int32(k)).wait_recv()
        total = total + tsums[k]
    sums_out[0:2, :] = stat[0:2, :]
    sums_out[2:3, :] = total[0:8].sum(0, keepdims=True) / D
    sums_out[3:4, :] = total[8:16].sum(0, keepdims=True) / D
    sums_out[4:8, :] = jnp.zeros((4, TOK), F32)
    own_gh.wait()

    @pl.loop(1, N)
    def _(k):
        gh_copy(k).wait_recv()

    for part in range(NP):
        pass_copy(part, jnp.int32(0)).wait_recv()
        pass_copy(part, jnp.int32(0)).wait_send()
        half_copy(part).wait_send()

        @pl.loop(1, 8)
        def _(k):
            pass_copy(part, k).wait_recv()
            pass_copy(part, k).wait_send()
            fin_copy(part, k).wait_send()
            z_copy(part, k).wait_send()

        @pl.loop(1, N)
        def _(k):
            tok_copy(k, part).wait_send()

    @pl.loop(1, N)
    def _(k):
        gt_copy(k).wait_recv()
        sum_copy(k).wait_send()
        stat_copy(k).wait_send()
        gh_copy(k).wait_send()
        gg_copy(k).wait_send()
        gt_copy(k).wait_send()

    cot_copy(jnp.int32(1)).wait_send()
    cot_copy(jnp.int32(8)).wait_send()
    cot_forward(jnp.int32(8)).wait_send()

    @pl.loop(1, 4)
    def _(j):
        cot_copy(2 * j).wait_send()
        cot_along_x(j).wait_send()
        cot_along_y(j).wait_send()
        cot_forward(2 * j).wait_send()
        cot_forward(8 + 2 * j).wait_send()


def finish(x, ghT, gain, sums, gw, gb, out, gw_out, gain_out, bias_out, col):
    t = pl.program_id(0)

    @pl.when(t == 0)
    def _():
        for j, total in enumerate((gain_out, bias_out)):
            total[...] = jnp.zeros_like(total)
            for m in range(N):
                at = 29 * (m // 4) + 7 * (m % 4)
                total[at:at + 8, :] += gb[m, 8 * j:8 * j + 8, :]
        for j in range(4):
            col[j] = jnp.broadcast_to(sums[j:j + 1, :], (TOK, TOK)).T

    gw_out[...] = gw[...]

    def piece(at, n):
        g = ghT[pl.ds(at, n), :].T
        for u in range(n // 128):
            tile = pl.ds(at + u * 128, 128)
            scaled = g[:, u * 128:u * 128 + 128].astype(F32) * gain[pl.ds(t * (COLS // 128) + at // 128 + u, 1), :]
            normed = (x[:, tile].astype(F32) - col[0]) * col[1]
            out[:, tile] = (col[1] * (scaled - col[2] - normed * col[3])).astype(BF)

    @pl.loop(0, COLS // 512)
    def _(i):
        piece(pl.multiple_of(i * 512, 512), 512)

    piece(COLS // 512 * 512, COLS % 512)


def body(tokens, cotangent, kv_weight, gain, bias):
    V = pl.BlockSpec(memory_space=pltpu.VMEM)
    half = SH // 2
    scratch = [
        pltpu.VMEM((TOK, D), BF),
        pltpu.VMEM((SH, KVW), BF),
        pltpu.VMEM((D, TOK), BF),
        pltpu.VMEM((N, SH, TOK), BF),
        pltpu.VMEM((N * TOK, KVW), BF),
        pltpu.VMEM((8, TOK), F32),
        pltpu.VMEM((N, 8, TOK), F32),
        pltpu.VMEM((max(SIZE), N * TOK), BF),
        pltpu.VMEM((N, SH, TOK), BF),
        pltpu.VMEM((8, SH, 128), BF),
        pltpu.VMEM((8, half, 128), BF),
        pltpu.VMEM((8, half, 128), BF),
        pltpu.VMEM((8, half, 128), BF),
        pltpu.VMEM((half, 128), BF),
        pltpu.VMEM((1024, TOK), F32),
        pltpu.VMEM((1024, TOK), F32),
        pltpu.VMEM((2, 1024, TOK), F32),
        pltpu.VMEM((N, 128), F32),
        pltpu.VMEM((N, N, 128), F32),
        pltpu.VMEM((N, 128), F32),
        pltpu.VMEM((N, N, TOK), F32),
        pltpu.VMEM((N, N, TOK), F32),
    ]
    dma = pltpu.SemaphoreType.DMA
    sems = ([dma((N,))] * 2 + [dma((4,))] * 2 + [dma((NP, N))] * 2 + [dma((N,))] * 4 + [dma((NP,))] * 2
            + [dma((NP, 8))] * 6 + [dma((N,))] * 6 + [dma((5,))])
    gain, bias = gain.reshape(D // 128, 128), bias.reshape(D // 128, 128)
    A = pl.BlockSpec(memory_space=pl.ANY)
    ghT, gw, gb, sums = pl.pallas_call(
        kernel,
        out_shape=(
            jax.ShapeDtypeStruct((D, TOK), BF),
            jax.ShapeDtypeStruct((SH, KVW), BF),
            jax.ShapeDtypeStruct((N, N, 128), F32),
            jax.ShapeDtypeStruct((8, TOK), F32),
        ),
        in_specs=[A, V, A, V, V],
        out_specs=(A, V, V, V),
        scratch_shapes=scratch + sems,
        compiler_params=pltpu.CompilerParams(
            collective_id=0, has_side_effects=True, vmem_limit_bytes=60 << 20),
    )(tokens, cotangent, kv_weight, gain, bias)
    tile = pl.BlockSpec((TOK, COLS), lambda t: (0, t))
    turned = pl.BlockSpec((COLS, TOK), lambda t: (t, 0))
    weight = pl.BlockSpec((SH, KVW * COLS // D), lambda t: (0, t))
    out, gw, gain_sum, bias_sum = pl.pallas_call(
        finish,
        grid=(D // COLS,),
        out_shape=(
            jax.ShapeDtypeStruct((TOK, D), BF),
            jax.ShapeDtypeStruct((SH, KVW), BF),
            jax.ShapeDtypeStruct((D // 128, 128), F32),
            jax.ShapeDtypeStruct((D // 128, 128), F32),
        ),
        in_specs=[tile, turned, V, V, weight, V],
        out_specs=(tile, weight, V, V),
        scratch_shapes=[pltpu.VMEM((4, TOK, TOK), F32)],
        compiler_params=pltpu.CompilerParams(vmem_limit_bytes=60 << 20),
    )(tokens, ghT, gain, sums, gw, gb)
    return out, gw, gain_sum.reshape(D), bias_sum.reshape(D)


def solution(mesh):
    in_specs = (
        P(("replica", "outer"), None),
        P(("replica", "outer"), None),
        P("outer", None),
        P(),
        P(),
    )
    out_specs = (P(("replica", "outer"), None), P("outer", None), P(), P())
    return jax.shard_map(body, mesh=mesh, in_specs=in_specs, out_specs=out_specs, check_vma=False)
```

```python
import jax
import jax.numpy as jnp
from jax import lax
from jax.experimental import pallas as pl
from jax.experimental.pallas import tpu as pltpu
from jax.sharding import PartitionSpec as P

BF = jnp.bfloat16
F32 = jnp.float32
MESH = pl.DeviceIdType.MESH
EPS = 1e-05

D = 14848
TOK = 128
KVW = 1024
COLS = 3712
AHEAD = 2
GH_AT = 3
N = 16
SH = D // N
BASE = (0, 192, 384, 576, 768)
SIZE = (192, 192, 192, 192, 160)
HBASE = (0, 96, 192, 288, 384)
HALF = (96, 96, 96, 96, 80)
NP = 5


def div(a, b):
    return lax.div(a, jnp.int32(b))


def rem(a, b):
    return lax.rem(a, jnp.int32(b))


def kernel(x_hbm, cot, w_hbm, gain, bias, ghT, gw, gb, sums_out,
           x, w, xT, tok, cots, stat, stats, hid, ghs, s_buf, xr, zs, zr, fin,
           gcol, bcol, acc, gg, ggs, gtot, tsum, tsums,
           c_s, c_r, e_s, e_r, tk_s, tk_r, st_s, st_r, h_s, h_r, x_s, x_r, z_s, z_r, f_s, f_r, p_s, p_r,
           g_s, g_r, t_s, t_r, u_s, u_r, l_s):
    r = lax.axis_index("replica")
    o = lax.axis_index("outer")
    xlo, z = div(r, 8), rem(r, 8)
    xhi, y, c = div(o, 8), rem(div(o, 2), 4), rem(o, 2)

    def member(k, sign):
        dxh, dy, dc = div(k, 8), rem(div(k, 2), 4), rem(k, 2)
        xh = rem(xhi + dxh, 2)
        yy = rem(y + 4 + sign * dy, 4)
        cc = rem(c + dc, 2)
        xl = rem(xlo + dxh, 2)
        return xl * 8 + z, xh * 8 + yy * 2 + cc

    def ahead(k):
        return member(k, 1)

    def behind(k):
        return member(k, -1)

    def replica(k, sign):
        return rem(xlo + div(k, 8), 2) * 8 + rem(z + 8 + sign * rem(k, 8), 8), o

    bar = pltpu.get_barrier_semaphore()

    @pl.loop(1, N)
    def _(k):
        pl.semaphore_signal(bar, inc=1, device_id=ahead(k), device_id_type=MESH)
        pl.semaphore_signal(bar, inc=1, device_id=replica(k, 1), device_id_type=MESH)

    def remote(src, dst, ss, rs, dev):
        return pltpu.make_async_remote_copy(
            src_ref=src, dst_ref=dst, send_sem=ss, recv_sem=rs, device_id=dev, device_id_type=MESH)

    def rows(k, n=TOK):
        return pl.ds(pl.multiple_of(k * n, n), n)

    x_in = pltpu.make_async_copy(x_hbm, x, l_s.at[3])
    x_in.start()
    w_in = pltpu.make_async_copy(w_hbm, w, l_s.at[4])
    w_in.start()

    def cot_copy(k):
        return remote(cot, cots.at[rows(k)], c_s.at[k], c_r.at[k], ahead(k))

    def cot_along_y(j):
        at = pl.multiple_of((8 + 2 * j) * TOK, TOK)
        return remote(cots.at[pl.ds(8 * TOK, TOK // 2)], cots.at[pl.ds(at, TOK // 2)],
                      c_s.at[8 + 2 * j], c_r.at[8 + 2 * j], ahead(2 * j))

    def cot_along_x(j):
        at = pl.multiple_of((8 + 2 * j) * TOK + TOK // 2, TOK // 2)
        here = pl.multiple_of(2 * j * TOK + TOK // 2, TOK // 2)
        return remote(cots.at[pl.ds(here, TOK // 2)], cots.at[pl.ds(at, TOK // 2)],
                      e_s.at[j], e_r.at[j], ahead(jnp.int32(8)))

    def cot_forward(k):
        return remote(cots.at[rows(k)], cots.at[rows(k + 1)], c_s.at[k + 1], c_r.at[k + 1], ahead(jnp.int32(1)))

    own_cot = pltpu.make_async_copy(cot, cots.at[pl.ds(0, TOK)], l_s.at[0])
    own_cot.start()

    pl.semaphore_wait(bar, 2 * (N - 1))
    cot_copy(jnp.int32(8)).start()
    cot_copy(jnp.int32(1)).start()

    @pl.loop(1, 4)
    def _(j):
        cot_copy(2 * j).start()

    x_in.wait()

    def turn(t, total):
        s = pl.multiple_of(t * 512, 512)
        v = x[:, pl.ds(s, 512)].T
        xT[pl.ds(s, 512), :] = v
        return total + v.astype(F32).reshape(64, 8, TOK).sum(0)

    total = lax.fori_loop(0, D // 512, turn, jnp.zeros((8, TOK), F32))
    mean = total.sum(0, keepdims=True) / D

    def tok_copy(k, part):
        dev = ahead(k)
        at = pl.multiple_of(dev[1] * SH + BASE[part], 16)
        return remote(xT.at[pl.ds(at, SIZE[part])], tok.at[k, pl.ds(BASE[part], SIZE[part])],
                      tk_s.at[part, k], tk_r.at[part, k], dev)

    own_tok = pltpu.make_async_copy(xT.at[rows(o, SH)], tok.at[0], l_s.at[1])
    own_tok.start()
    def tok_start(part):
        @pl.loop(1, N)
        def _(k):
            tok_copy(k, part).start()

    for part in range(AHEAD):
        tok_start(part)

    def spread(t, total):
        s = pl.multiple_of(t * 512, 512)
        v = xT[pl.ds(s, 512), :].astype(F32) - mean
        return total + (v * v).reshape(64, 8, TOK).sum(0)

    total = lax.fori_loop(0, D // 512, spread, jnp.zeros((8, TOK), F32))
    inv = lax.rsqrt(total.sum(0, keepdims=True) / D + EPS)
    stat[0:1, :] = mean
    stat[1:2, :] = inv
    stats[0, 0:1, :] = mean
    stats[0, 1:2, :] = inv

    def stat_copy(k):
        return remote(stat, stats.at[k], st_s.at[k], st_r.at[k], ahead(k))

    @pl.loop(1, N)
    def _(k):
        stat_copy(k).start()

    first_tile = div(o * SH, 128)
    shift = pl.multiple_of(rem(o, 4) * 32, 32)
    for t in range(8):
        gcol[t * 128:t * 128 + 128, :] = jnp.broadcast_to(gain[pl.ds(first_tile + t, 1), :], (TOK, 128)).T
        bcol[t * 128:t * 128 + 128, :] = jnp.broadcast_to(bias[pl.ds(first_tile + t, 1), :], (TOK, 128)).T

    cot_copy(jnp.int32(8)).wait_recv()

    @pl.loop(1, 4)
    def _(j):
        cot_along_y(j).start()

    cot_forward(jnp.int32(8)).start()

    @pl.loop(1, 4)
    def _(j):
        cot_copy(2 * j).wait_recv()
        cot_along_x(j).start()
        cot_forward(2 * j).start()

    @pl.loop(1, 4)
    def _(j):
        cot_along_y(j).wait_recv()
        cot_along_x(j).wait_recv()
        cot_forward(8 + 2 * j).start()

    own_cot.wait()
    w_in.wait()
    tsum[...] = jnp.zeros_like(tsum)

    own_tok.wait()
    acc[...] = jnp.zeros_like(acc)

    def gh_copy(k):
        return remote(ghs.at[k], ghT.at[rows(o, SH)], h_s.at[k], h_r.at[k], behind(k))

    beside = replica(jnp.int32(8), 1)

    def half_copy(part):
        h = HALF[part]
        at = pl.multiple_of(BASE[part] + (1 - xlo) * h, 16)
        return remote(s_buf.at[:, pl.ds(at, h)], xr.at[:, pl.ds(HBASE[part], h)], x_s.at[part], x_r.at[part], beside)

    def z_copy(part, k):
        at = pl.ds(HBASE[part], HALF[part])
        return remote(zs.at[rem(z + k, 8), at], zr.at[k, at], z_s.at[part, k], z_r.at[part, k], replica(k, 1))

    def gw_at(part, zz):
        return gw.at[pl.ds(pl.multiple_of(BASE[part] + xlo * HALF[part], 16), HALF[part]), rows(zz)]

    def fin_copy(part, k):
        return remote(fin.at[pl.ds(HBASE[part], HALF[part])], gw_at(part, z), f_s.at[part, k], f_r.at[part, k],
                      replica(k, 1))

    def pass_copy(part, k):
        here = gw_at(part, rem(z + 8 - k, 8))
        return remote(here, here, p_s.at[part, k], p_r.at[part, k], beside)

    def receive_part(part):
        @pl.loop(1, N)
        def _(k):
            tok_copy(k, part).wait_recv()
            if part == 0:
                stat_copy(k).wait_recv()
            if part + AHEAD < NP:
                tok_copy(k, part + AHEAD).start()
            if part == GH_AT:
                gh_copy(k).start()

    def weight_part(part):
        base, size = BASE[part], SIZE[part]

        step = size // 2
        for u in range(2):
            lo = base + u * step

            def block(k, carry):
                ag, ab = carry
                normed = (tok[k, lo:lo + step, :].astype(F32) - stats[k, 0:1, :]) * stats[k, 1:2, :]
                at = pl.multiple_of(shift + lo, 16)
                hid[u * step:(u + 1) * step, rows(k)] = (
                    gcol[pl.ds(at, step), :] * normed + bcol[pl.ds(at, step), :]).astype(BF)
                gh = ghs[k, lo:lo + step, :].astype(F32)
                scaled = gcol[pl.ds(at, step), :] * gh
                tsum[k, 0:8, :] += scaled.reshape(step // 8, 8, TOK).sum(0)
                tsum[k, 8:16, :] += (scaled * normed).reshape(step // 8, 8, TOK).sum(0)
                return ag + gh * normed, ab + gh

            zero = jnp.zeros((step, TOK), F32)
            ag, ab = lax.fori_loop(0, N, block, (zero, zero))
            at = pl.multiple_of(shift + lo, 16)
            acc[0, pl.ds(at, step), :] = ag
            acc[1, pl.ds(at, step), :] = ab

        @pl.loop(0, 4)
        def _(n):
            v = jnp.dot(hid[0:size, :], cots[:, rows(n, 256)], preferred_element_type=F32).astype(BF)
            s_buf[2 * n, base:base + size, :] = v[:, :128]
            s_buf[2 * n + 1, base:base + size, :] = v[:, 128:]

        half_copy(part).start()

    def beside_part(part):
        h, hb = HALF[part], HBASE[part]
        half_copy(part).wait_recv()
        at = pl.multiple_of(BASE[part] + xlo * h, 16)
        for n in range(8):
            zs[n, hb:hb + h, :] = (
                s_buf[n, pl.ds(at, h), :].astype(F32) + xr[n, hb:hb + h, :].astype(F32)).astype(BF)

        @pl.loop(1, 8)
        def _(k):
            z_copy(part, k).start()

    def own_part(part):
        h, hb = HALF[part], HBASE[part]

        @pl.loop(1, 8)
        def _(k):
            z_copy(part, k).wait_recv()

        at = pl.multiple_of(BASE[part] + xlo * h, 16)
        v = s_buf[z, pl.ds(at, h), :].astype(F32) + xr[z, hb:hb + h, :].astype(F32)
        for k in range(1, 8):
            v = v + zr[k, hb:hb + h, :].astype(F32)
        v = (v / N).astype(BF)
        fin[hb:hb + h, :] = v
        gw[pl.ds(at, h), rows(z)] = v

        @pl.loop(1, 8)
        def _(k):
            fin_copy(part, k).start()

        pass_copy(part, jnp.int32(0)).start()

    def pass_part(part):
        @pl.loop(1, 8)
        def _(k):
            fin_copy(part, k).wait_recv()
            pass_copy(part, k).start()

    def gg_copy(k):
        return remote(gg, ggs.at[r], g_s.at[k], g_r.at[k], replica(k, 1))

    def sum_copy(k):
        return remote(tsum.at[k], tsums.at[k], u_s.at[k], u_r.at[k], behind(k))

    def gt_copy(k):
        return remote(gtot, gb.at[o], t_s.at[k], t_r.at[k], ahead(k))

    receive_part(0)

    @pl.loop(0, 8)
    def _(j):
        @pl.when(j == 0)
        def _():
            cot_copy(jnp.int32(1)).wait_recv()

        @pl.when(j > 0)
        def _():
            cot_forward(2 * j).wait_recv()

        v = lax.dot_general(w[...], cots[rows(j, 2 * TOK), :], (((1,), (1,)), ((), ())),
                            preferred_element_type=F32).astype(BF)
        ghs[2 * j] = v[:, :TOK]
        ghs[2 * j + 1] = v[:, TOK:]

    own_gh = pltpu.make_async_copy(ghs.at[0], ghT.at[rows(o, SH)], l_s.at[2])
    own_gh.start()

    for i in range(NP + 3):
        if i < NP:
            if i > 0:
                receive_part(i)
            weight_part(i)
        if i == NP - 1:
            for j in (0, 1):
                for t in range(8):
                    gg[j * 8 + t:j * 8 + t + 1, :] = acc[j, t * 128:t * 128 + 128, :].T.sum(0, keepdims=True)
            ggs[r] = gg[...]

            @pl.loop(1, N)
            def _(k):
                sum_copy(k).start()
                gg_copy(k).start()
        if 0 <= i - 1 < NP:
            beside_part(i - 1)
        if 0 <= i - 2 < NP:
            own_part(i - 2)
        if 0 <= i - 3 < NP:
            pass_part(i - 3)
        if i == NP:
            @pl.loop(1, N)
            def _(k):
                gg_copy(k).wait_recv()

            gtot[...] = ggs[...].sum(0) / N
            gb[o] = gtot[...]

            @pl.loop(1, N)
            def _(k):
                gt_copy(k).start()

    total = tsum[0]
    for k in range(1, N):
        sum_copy(jnp.int32(k)).wait_recv()
        total = total + tsums[k]
    sums_out[0:2, :] = stat[0:2, :]
    sums_out[2:3, :] = total[0:8].sum(0, keepdims=True) / D
    sums_out[3:4, :] = total[8:16].sum(0, keepdims=True) / D
    sums_out[4:8, :] = jnp.zeros((4, TOK), F32)
    own_gh.wait()

    @pl.loop(1, N)
    def _(k):
        gh_copy(k).wait_recv()

    for part in range(NP):
        pass_copy(part, jnp.int32(0)).wait_recv()
        pass_copy(part, jnp.int32(0)).wait_send()
        half_copy(part).wait_send()

        @pl.loop(1, 8)
        def _(k):
            pass_copy(part, k).wait_recv()
            pass_copy(part, k).wait_send()
            fin_copy(part, k).wait_send()
            z_copy(part, k).wait_send()

        @pl.loop(1, N)
        def _(k):
            tok_copy(k, part).wait_send()

    @pl.loop(1, N)
    def _(k):
        gt_copy(k).wait_recv()
        sum_copy(k).wait_send()
        stat_copy(k).wait_send()
        gh_copy(k).wait_send()
        gg_copy(k).wait_send()
        gt_copy(k).wait_send()

    cot_copy(jnp.int32(1)).wait_send()
    cot_copy(jnp.int32(8)).wait_send()
    cot_forward(jnp.int32(8)).wait_send()

    @pl.loop(1, 4)
    def _(j):
        cot_copy(2 * j).wait_send()
        cot_along_x(j).wait_send()
        cot_along_y(j).wait_send()
        cot_forward(2 * j).wait_send()
        cot_forward(8 + 2 * j).wait_send()


def finish(x, ghT, gain, sums, gw, gb, out, gw_out, gain_out, bias_out, col):
    t = pl.program_id(0)

    @pl.when(t == 0)
    def _():
        for j, total in enumerate((gain_out, bias_out)):
            total[...] = jnp.zeros_like(total)
            for m in range(N):
                at = 29 * (m // 4) + 7 * (m % 4)
                total[at:at + 8, :] += gb[m, 8 * j:8 * j + 8, :]
        for j in range(4):
            col[j] = jnp.broadcast_to(sums[j:j + 1, :], (TOK, TOK)).T

    gw_out[...] = gw[...]

    def piece(at, n):
        g = ghT[pl.ds(at, n), :].T
        for u in range(n // 128):
            tile = pl.ds(at + u * 128, 128)
            scaled = g[:, u * 128:u * 128 + 128].astype(F32) * gain[pl.ds(t * (COLS // 128) + at // 128 + u, 1), :]
            normed = (x[:, tile].astype(F32) - col[0]) * col[1]
            out[:, tile] = (col[1] * (scaled - col[2] - normed * col[3])).astype(BF)

    @pl.loop(0, COLS // 512)
    def _(i):
        piece(pl.multiple_of(i * 512, 512), 512)

    piece(COLS // 512 * 512, COLS % 512)


def body(tokens, cotangent, kv_weight, gain, bias):
    V = pl.BlockSpec(memory_space=pltpu.VMEM)
    half = SH // 2
    scratch = [
        pltpu.VMEM((TOK, D), BF),
        pltpu.VMEM((SH, KVW), BF),
        pltpu.VMEM((D, TOK), BF),
        pltpu.VMEM((N, SH, TOK), BF),
        pltpu.VMEM((N * TOK, KVW), BF),
        pltpu.VMEM((8, TOK), F32),
        pltpu.VMEM((N, 8, TOK), F32),
        pltpu.VMEM((max(SIZE), N * TOK), BF),
        pltpu.VMEM((N, SH, TOK), BF),
        pltpu.VMEM((8, SH, 128), BF),
        pltpu.VMEM((8, half, 128), BF),
        pltpu.VMEM((8, half, 128), BF),
        pltpu.VMEM((8, half, 128), BF),
        pltpu.VMEM((half, 128), BF),
        pltpu.VMEM((1024, TOK), F32),
        pltpu.VMEM((1024, TOK), F32),
        pltpu.VMEM((2, 1024, TOK), F32),
        pltpu.VMEM((N, 128), F32),
        pltpu.VMEM((N, N, 128), F32),
        pltpu.VMEM((N, 128), F32),
        pltpu.VMEM((N, N, TOK), F32),
        pltpu.VMEM((N, N, TOK), F32),
    ]
    dma = pltpu.SemaphoreType.DMA
    sems = ([dma((N,))] * 2 + [dma((4,))] * 2 + [dma((NP, N))] * 2 + [dma((N,))] * 4 + [dma((NP,))] * 2
            + [dma((NP, 8))] * 6 + [dma((N,))] * 6 + [dma((5,))])
    gain, bias = gain.reshape(D // 128, 128), bias.reshape(D // 128, 128)
    A = pl.BlockSpec(memory_space=pl.ANY)
    ghT, gw, gb, sums = pl.pallas_call(
        kernel,
        out_shape=(
            jax.ShapeDtypeStruct((D, TOK), BF),
            jax.ShapeDtypeStruct((SH, KVW), BF),
            jax.ShapeDtypeStruct((N, N, 128), F32),
            jax.ShapeDtypeStruct((8, TOK), F32),
        ),
        in_specs=[A, V, A, V, V],
        out_specs=(A, V, V, V),
        scratch_shapes=scratch + sems,
        compiler_params=pltpu.CompilerParams(
            collective_id=0, has_side_effects=True, vmem_limit_bytes=60 << 20),
    )(tokens, cotangent, kv_weight, gain, bias)
    tile = pl.BlockSpec((TOK, COLS), lambda t: (0, t))
    turned = pl.BlockSpec((COLS, TOK), lambda t: (t, 0))
    weight = pl.BlockSpec((SH, KVW * COLS // D), lambda t: (0, t))
    out, gw, gain_sum, bias_sum = pl.pallas_call(
        finish,
        grid=(D // COLS,),
        out_shape=(
            jax.ShapeDtypeStruct((TOK, D), BF),
            jax.ShapeDtypeStruct((SH, KVW), BF),
            jax.ShapeDtypeStruct((D // 128, 128), F32),
            jax.ShapeDtypeStruct((D // 128, 128), F32),
        ),
        in_specs=[tile, turned, V, V, weight, V],
        out_specs=(tile, weight, V, V),
        scratch_shapes=[pltpu.VMEM((4, TOK, TOK), F32)],
        compiler_params=pltpu.CompilerParams(vmem_limit_bytes=60 << 20),
    )(tokens, ghT, gain, sums, gw, gb)
    return out, gw, gain_sum.reshape(D), bias_sum.reshape(D)


def solution(mesh):
    in_specs = (
        P(("replica", "outer"), None),
        P(("replica", "outer"), None),
        P("outer", None),
        P(),
        P(),
    )
    out_specs = (P(("replica", "outer"), None), P("outer", None), P(), P())
    return jax.shard_map(body, mesh=mesh, in_specs=in_specs, out_specs=out_specs, check_vma=False)
```
